32 devices in a mesh: groups: 2 (over x), slot: 8 (over z, y), tensor: 2 (over core).
Axes of the slice: x: 2, y: 2, z: 4, core: 2. Of those that a mesh axis runs over, the one named last changes fastest.
Arguments:
- tokens: bfloat16 [1024, 3072], P(('groups', 'slot'), 'tensor'), parts along dimension 0, may hold values from -6 to 6
- expert_ids: int32 [1024, 2], P(('groups', 'slot')), parts along dimension 0, may hold values from 0 to 3, all different within a row; in each aligned block of 64 rows (0 to 63, 64 to 127, ...) at most 48 rows name the same one
- route_weights: float32 [1024, 2], P(('groups', 'slot')), parts along dimension 0, may hold values from 0.2 to 1
- up_weight: bfloat16 [8, 3072, 8192], P('slot', None, 'tensor'), as said below
- down_weight: bfloat16 [8, 8192, 3072], P('slot', 'tensor'), as said below
Outputs:
- mixed: bfloat16 [1024, 3072], P(('groups', 'slot'), 'tensor'), parts along dimension 0
The draws below stay inside these ranges and needn't reach their ends.
There are 2 independent parts, one for each index of `groups`. The reference program is written for one: setup_inputs(seed, part) draws one part's arguments, and reference() takes and returns one part's arrays. A program takes and returns all parts, laid end to end along the dimension named above; an argument that names none is the same for every part. Nothing has to cross between parts.
Inputs may be any that keep to these rules, and one draw needn't show every extreme that they name: `expert_ids`: each row names 2 different experts; among the tokens of one slot index no expert is named by more than 48 rows, a bound that some expert reaches in some of these blocks. `up_weight`: the slices of copy 2 e + 1 hold the same numbers as those of copy 2 e. `down_weight`: the slices of copy 2 e + 1 hold the same numbers as those of copy 2 e.
All inputs are finite; a program needn't handle non-finite values.
Results may differ from the reference program's by a relative error of at most 0.005.
Values may be sent and summed in bfloat16 or wider, within the bound.
A program may use at most 128 MiB of HBM per device.

```python
import math
import jax
import jax.numpy as jnp
import numpy as np

E = 4
TOPK = 2
D = 3072
FF = 8192
TOK_DEV = 64
MOST = 48
COPIES = 8
SUBS = 1
FSL = 8192
TOKENS = 512
N_SLOT = 8


def draw_up_weight(key, part):
    key = jax.random.fold_in(key, 11)
    base = jax.random.normal(key, (E, D, FF), jnp.float32) * D ** (-0.5)
    copies = jnp.repeat(base, 2, axis=0).reshape(COPIES, D, SUBS, FSL)
    return jnp.transpose(copies, (0, 2, 1, 3)).reshape(COPIES * SUBS, D, FSL).astype(jnp.bfloat16)


def draw_down_weight(key, part):
    key = jax.random.fold_in(key, 23)
    base = jax.random.normal(key, (E, FF, D), jnp.float32) * FF ** (-0.5)
    copies = jnp.repeat(base, 2, axis=0)
    return copies.reshape(COPIES * SUBS, FSL, D).astype(jnp.bfloat16)


def level_of(key, shape, pieces, smallest, top_value):
    gain, own = 1.0, jax.random.fold_in(key, 6)
    for dim, parts in pieces:
        draws = jnp.exp(jax.random.uniform(jax.random.fold_in(own, dim), (parts,), jnp.float32, smallest / len(pieces), top_value / len(pieces)))
        gain = gain * jnp.repeat(draws, shape[dim] // parts).reshape([-1 if axis == dim else 1 for axis in range(len(shape))])
    return gain


def assign_block(key, own, number, rows, number_of, top, limit, slope):
    sequence = jax.random.permutation(key, number_of)
    crowded, usual = portions_of(number_of, rows * top, limit, slope, True), portions_of(number_of, rows * top, limit, slope, False)
    places = jnp.arange(number_of)

    def named(tallies, offset_by):
        used = int((tallies > 0).sum())
        fixed = max(1, used // 4)
        passed = fixed + (places - fixed + offset_by * (used - fixed)) % max(1, number_of - fixed)
        return jnp.zeros((number_of,), jnp.int32).at[sequence[jnp.where(places < fixed, places, passed)]].set(jnp.asarray(tallies, jnp.int32))

    tallies = jnp.where(number % 4 == 0, named(crowded, number // 4), named(usual, number - number // 4 - 1))
    mixed = jax.random.permutation(jax.random.fold_in(own, 3), number_of)
    source_of, sink = mixed[0:number_of // 2 * 2:2], mixed[1:number_of // 2 * 2:2]
    margin = jnp.minimum(tallies[source_of] - 1, limit - tallies[sink]) // 2
    margin = jnp.where((source_of == sequence[0]) | (sink == sequence[0]) | (tallies[sink] == 0), 0, jnp.maximum(margin, 0))
    passed = jax.random.randint(jax.random.fold_in(own, 4), (number_of // 2,), 0, 1 << 20) % (margin + 1)
    tallies = tallies.at[source_of].add(-passed).at[sink].add(passed)
    items = jnp.searchsorted(jnp.cumsum(tallies), jnp.arange(rows * top), side="right").astype(jnp.int32)
    table = items.reshape(top, rows).T
    table = table[jax.random.permutation(jax.random.fold_in(own, 1), rows)]
    offset_by = jax.random.randint(jax.random.fold_in(own, 2), (rows, 1), 0, top)
    return jnp.take_along_axis(table, (jnp.arange(top)[None, :] + offset_by) % top, axis=1)


def portions_of(count, total, most, lean, full):
    portions = [(1 << 20) // math.isqrt(grade ** lean) + 1 for grade in range(1, count + 1)]
    largest = most if full else min(most, max(-(-total // count), total * portions[0] // sum(portions)))
    least = 1 if total - largest >= count - 1 else 0
    counts, rest = [largest] + [least] * (count - 1), total - largest - least * (count - 1)
    while rest > 0:
        free = [i for i in range(1, count) if counts[i] < largest] or [i for i in range(1, count) if counts[i] < most]
        mass, budget = sum([portions[i] for i in free]), rest
        for i in free:
            more = min(most - counts[i], max(1, budget * portions[i] // mass), rest)
            counts[i] = counts[i] + more
            rest = rest - more
    return np.array(counts)


def gaussian(key, extent, scale, reach, pieces=(), dtype=jnp.bfloat16):
    array = scale * jax.random.normal(key, extent, jnp.float32)
    if pieces:
        array = array * level_of(key, extent, pieces, -0.22, 0.18)
    return jnp.clip(array, -reach, reach).astype(dtype)


def setup_inputs(seed: int = 0, part: int = 0) -> dict:
    key_of = jax.random.split(jax.random.key(seed), 6)
    part_splits = jax.random.split(jax.random.fold_in(key_of[5], part), 6)
    tokens = gaussian(part_splits[0], (TOKENS, D), 1.0, 6.0, ((0, 8), (1, 2)))
    expert_ids_keys = jax.random.split(jax.random.fold_in(part_splits[1], 1), TOKENS // TOK_DEV)
    expert_ids_turns = jax.random.permutation(jax.random.fold_in(part_splits[1], 3), TOKENS // TOK_DEV)
    expert_ids = jax.vmap(lambda own, number: assign_block(jax.random.fold_in(part_splits[1], 2), own, number, TOK_DEV, E, TOPK, MOST, 2))(expert_ids_keys, expert_ids_turns).reshape((TOKENS, TOPK))
    route_weights = jnp.clip(0.2 + 0.8 * jax.random.uniform(part_splits[2], (TOKENS, TOPK), jnp.float32) ** level_of(part_splits[2], (TOKENS, TOPK), ((0, 8),), -0.2, 0.2), 0.2, 1.0)
    up_weight = draw_up_weight(jax.random.fold_in(key_of[5], 71), part)
    down_weight = draw_down_weight(jax.random.fold_in(key_of[5], 71), part)
    return {"tokens": tokens, "expert_ids": expert_ids, "route_weights": route_weights, "up_weight": up_weight, "down_weight": down_weight}


def reference(tokens, expert_ids, route_weights, up_weight, down_weight):
    up_copies = up_weight.reshape(COPIES, SUBS, D, FSL)
    down_copies = down_weight.reshape(COPIES, SUBS * FSL, D)
    combined = jnp.zeros((TOKENS, D), jnp.float32)
    row_limit = N_SLOT * MOST
    for expert in range(E):
        expert_up = jnp.transpose(up_copies[2 * expert], (1, 0, 2)).reshape(D, SUBS * FSL)
        expert_down = down_copies[2 * expert]
        chosen = expert_ids == expert
        gate_weight = jnp.sum(jnp.where(chosen, route_weights, jnp.zeros_like(route_weights)), axis=1)
        picked = jnp.any(chosen, axis=1)
        row_index = jnp.nonzero(picked, size=row_limit, fill_value=0)[0].astype(jnp.int32)
        is_valid = jnp.arange(row_limit) < jnp.sum(picked.astype(jnp.int32))
        picked_rows = tokens[row_index]
        hidden = jax.nn.silu(jnp.dot(picked_rows, expert_up, preferred_element_type=jnp.float32)).astype(jnp.bfloat16)
        result = jnp.dot(hidden, expert_down, preferred_element_type=jnp.float32)
        factor = jnp.where(is_valid, gate_weight[row_index], jnp.zeros_like(gate_weight[row_index]))
        combined = combined.at[row_index].add(factor[:, None] * result)
    return combined.astype(jnp.bfloat16)
```

```python
import functools

import jax
import jax.numpy as jnp
from jax import lax
from jax.experimental import pallas as pl
from jax.experimental.pallas import tpu as pltpu
from jax.sharding import PartitionSpec as P

E = 4
CAP = 24
MOST = 48
WIDTH = 256
UP_SLOTS = 4
UP_TILE = 512
MESH = pl.DeviceIdType.MESH


def fused_kernel(
    tok_ref, ids_ref, weight_ref, up_hbm, down_hbm, out_ref,
    packed, x_own, x_sib, up_buf, down_buf, acc, hid, part_out, part_own, part_in, summed, returned,
    up_sem, down_sem, go_send, go_recv, fwd_send, fwd_recv, part_send, part_recv, back_send, back_recv,
):
    tok_rows, half = tok_ref.shape
    chunks = half // WIDTH
    rows = E * MOST
    hidden_units = acc.shape[1]
    slot = lax.axis_index("slot")
    core = lax.axis_index("tensor")
    mine = slot // 2
    lane = lax.rem(slot, 2)
    sibling = 1 - core

    def up_copies(c):
        place = lax.rem(c, UP_SLOTS)
        return [
            pltpu.make_async_copy(
                up_hbm.at[0, pl.ds(pl.multiple_of(side * half + c * WIDTH, WIDTH), WIDTH), :],
                up_buf.at[place, i],
                up_sem.at[place, i],
            )
            for i, side in enumerate((core, sibling))
        ]

    def down_copies(c):
        return [
            pltpu.make_async_copy(
                down_hbm.at[0, :, pl.ds(pl.multiple_of(side * half + c * WIDTH, WIDTH), WIDTH)],
                down_buf.at[c, i],
                down_sem.at[c, i],
            )
            for i, side in enumerate((sibling, core))
        ]

    def peer(k):
        return lax.rem(mine + k, E)

    def go_copy(c, k):
        return pltpu.make_async_remote_copy(
            src_ref=packed.at[c, peer(k)],
            dst_ref=x_own.at[c, mine],
            send_sem=go_send.at[c, k - 1],
            recv_sem=go_recv.at[c, k - 1],
            device_id={"slot": peer(k) * 2 + lane},
            device_id_type=MESH,
        )

    def fwd_copy(c):
        return pltpu.make_async_remote_copy(
            src_ref=x_own.at[c],
            dst_ref=x_sib.at[c],
            send_sem=fwd_send.at[c],
            recv_sem=fwd_recv.at[c],
            device_id={"tensor": sibling},
            device_id_type=MESH,
        )

    def part_copy(c):
        return pltpu.make_async_remote_copy(
            src_ref=part_out.at[c],
            dst_ref=part_in.at[c],
            send_sem=part_send.at[c],
            recv_sem=part_recv.at[c],
            device_id={"tensor": sibling},
            device_id_type=MESH,
        )

    def back_copy(c, k):
        return pltpu.make_async_remote_copy(
            src_ref=summed.at[c, peer(k)],
            dst_ref=returned.at[c, mine],
            send_sem=back_send.at[c, k - 1],
            recv_sem=back_recv.at[c, k - 1],
            device_id={"slot": peer(k) * 2 + lane},
            device_id_type=MESH,
        )

    barrier = pltpu.get_barrier_semaphore()
    for k in range(1, E):
        pl.semaphore_signal(barrier, inc=1, device_id={"slot": peer(k) * 2 + lane}, device_id_type=MESH)
    pl.semaphore_signal(barrier, inc=1, device_id={"tensor": sibling}, device_id_type=MESH)

    for c in range(UP_SLOTS):
        for copy in up_copies(c):
            copy.start()

    first, second = ids_ref[:, 0:1], ids_ref[:, 1:2]
    experts = lax.broadcasted_iota(jnp.int32, (tok_rows, 128), 1)
    is_first = jnp.where(experts == first, 1.0, 0.0)
    is_second = jnp.where(experts == second, 1.0, 0.0)
    before = jnp.where(
        lax.broadcasted_iota(jnp.int32, (tok_rows, tok_rows), 0)
        > lax.broadcasted_iota(jnp.int32, (tok_rows, tok_rows), 1),
        1.0,
        0.0,
    ).astype(jnp.bfloat16)
    rank = jnp.dot(before, (is_first + is_second).astype(jnp.bfloat16), preferred_element_type=jnp.float32)
    place = rank + (experts * MOST).astype(jnp.float32)
    columns = lax.broadcasted_iota(jnp.int32, (tok_rows, rows), 1).astype(jnp.float32)
    one_first = jnp.where(columns == jnp.sum(is_first * place, axis=1, keepdims=True), 1.0, 0.0)
    one_second = jnp.where(columns == jnp.sum(is_second * place, axis=1, keepdims=True), 1.0, 0.0)
    chosen = (one_first + one_second).T.astype(jnp.bfloat16)
    one_first = one_first.astype(jnp.bfloat16)
    one_second = one_second.astype(jnp.bfloat16)

    for c in range(chunks):
        piece = jnp.dot(
            chosen, tok_ref[:, c * WIDTH : (c + 1) * WIDTH], preferred_element_type=jnp.float32
        ).astype(jnp.bfloat16)
        packed[c] = piece.reshape(E, MOST, WIDTH)
    pl.semaphore_wait(barrier, E)
    for c in range(chunks):
        for k in range(1, E):
            go_copy(c, k).start()
    for c in range(chunks):
        x_own[c, mine] = packed[c, mine]

    def up_step(c, start, final):
        fwd_copy(c).wait_recv()
        for copy in up_copies(c):
            copy.wait()
        spot = lax.rem(c, UP_SLOTS)
        left = x_own[c].reshape(rows, WIDTH)
        right = x_sib[c].reshape(rows, WIDTH)

        @pl.loop(0, hidden_units // UP_TILE)
        def _(n):
            at = pl.ds(pl.multiple_of(n * UP_TILE, UP_TILE), UP_TILE)
            value = jnp.dot(left, up_buf[spot, 0, :, at], preferred_element_type=jnp.float32)
            value += jnp.dot(right, up_buf[spot, 1, :, at], preferred_element_type=jnp.float32)
            if not start:
                value += acc[:, at]
            if final:
                hid[:, at] = (value / (1.0 + jnp.exp(-value))).astype(jnp.bfloat16)
            else:
                acc[:, at] = value

        for copy in down_copies(c):
            copy.start()

    def arrive(c):
        for k in range(1, E):
            go_copy(c, k).wait_recv()
        fwd_copy(c).start()

    arrive(0)
    arrive(1)
    up_step(0, True, False)
    for copy in up_copies(UP_SLOTS):
        copy.start()

    @pl.loop(1, chunks - 1)
    def _(c):
        arrive(c + 1)
        up_step(c, False, False)

        @pl.when(c + UP_SLOTS < chunks)
        def _():
            for copy in up_copies(c + UP_SLOTS):
                copy.start()

    up_step(chunks - 1, False, True)

    def finish(c):
        part_copy(c).wait_recv()
        total = (part_own[c] + part_in[c]).astype(jnp.bfloat16)
        summed[c] = total.reshape(E, MOST, WIDTH)
        for k in range(1, E):
            back_copy(c, k).start()
        returned[c, mine] = summed[c, mine]

    @pl.loop(0, chunks)
    def _(c):
        for copy in down_copies(c):
            copy.wait()
        part_out[c] = jnp.dot(hid[...], down_buf[c, 0], preferred_element_type=jnp.float32)
        part_copy(c).start()
        part_own[c] = jnp.dot(hid[...], down_buf[c, 1], preferred_element_type=jnp.float32)

        @pl.when(c > 0)
        def _():
            finish(c - 1)

    finish(chunks - 1)

    for c in range(chunks):
        for k in range(1, E):
            back_copy(c, k).wait_recv()
        block = returned[c].reshape(rows, WIDTH)
        value = weight_ref[:, 0:1] * jnp.dot(one_first, block, preferred_element_type=jnp.float32)
        value += weight_ref[:, 1:2] * jnp.dot(one_second, block, preferred_element_type=jnp.float32)
        out_ref[:, c * WIDTH : (c + 1) * WIDTH] = value.astype(jnp.bfloat16)

    for c in range(chunks):
        fwd_copy(c).wait_send()
        part_copy(c).wait_send()
        for k in range(1, E):
            go_copy(c, k).wait_send()
            back_copy(c, k).wait_send()


def fused(tokens, expert_ids, route_weights, up_weight, down_weight):
    tok_rows, half = tokens.shape
    hidden_units = up_weight.shape[2]
    chunks = half // WIDTH
    rows = E * MOST
    vmem = pl.BlockSpec(memory_space=pltpu.VMEM)
    hbm = pl.BlockSpec(memory_space=pl.ANY)
    sems = lambda *shape: pltpu.SemaphoreType.DMA(shape)
    blocks = pltpu.VMEM((chunks, E, MOST, WIDTH), jnp.bfloat16)
    wide = pltpu.VMEM((chunks, rows, WIDTH), jnp.float32)
    return pl.pallas_call(
        fused_kernel,
        out_shape=jax.ShapeDtypeStruct((tok_rows, half), jnp.bfloat16),
        in_specs=[vmem, vmem, vmem, hbm, hbm],
        out_specs=vmem,
        scratch_shapes=[
            blocks,
            blocks,
            blocks,
            pltpu.VMEM((UP_SLOTS, 2, WIDTH, hidden_units), jnp.bfloat16),
            pltpu.VMEM((chunks, 2, hidden_units, WIDTH), jnp.bfloat16),
            pltpu.VMEM((rows, hidden_units), jnp.float32),
            pltpu.VMEM((rows, hidden_units), jnp.bfloat16),
            wide,
            wide,
            wide,
            blocks,
            blocks,
            sems(UP_SLOTS, 2),
            sems(chunks, 2),
            sems(chunks, E - 1),
            sems(chunks, E - 1),
            sems(chunks),
            sems(chunks),
            sems(chunks),
            sems(chunks),
            sems(chunks, E - 1),
            sems(chunks, E - 1),
        ],
        compiler_params=pltpu.CompilerParams(
            collective_id=0, has_side_effects=True, vmem_limit_bytes=60 * 1024 * 1024
        ),
        cost_estimate=pl.CostEstimate(
            flops=8 * rows * half * hidden_units,
            bytes_accessed=8 * half * hidden_units,
            transcendentals=rows * hidden_units,
        ),
    )(tokens, expert_ids, route_weights, up_weight, down_weight)


def shards(tokens, expert_ids, route_weights, up_weight, down_weight):
    slot_count = lax.axis_size("slot")
    tok_rows = tokens.shape[0]
    copy_count = 2 * E
    sub_count = slot_count // copy_count
    up_matrix = up_weight[0]
    down_matrix = down_weight[0]
    flat_ids = expert_ids.reshape(-1)
    one_hot = (flat_ids[:, None] == jnp.arange(E, dtype=jnp.int32)[None, :]).astype(jnp.int32)
    route_rank = jnp.sum(one_hot * (jnp.cumsum(one_hot, axis=0) - 1), axis=1)
    overflow = (route_rank >= CAP).astype(jnp.int32)
    target = ((2 * flat_ids + overflow) * CAP + route_rank - overflow * CAP).reshape(
        tok_rows, expert_ids.shape[1]
    )
    positions = jnp.arange(copy_count * CAP, dtype=jnp.int32)
    matches = target[None, :, :] == positions[:, None, None]
    chosen = jnp.sum(matches.astype(jnp.float32), axis=2).astype(jnp.bfloat16)
    scaled = jnp.sum(
        jnp.where(matches, route_weights[None, :, :], jnp.zeros_like(route_weights)[None, :, :]),
        axis=2,
    )
    gathered = lax.all_gather(tokens, "tensor", axis=1, tiled=True)
    packed = jnp.dot(chosen, gathered, preferred_element_type=jnp.float32).astype(jnp.bfloat16)
    feature_width = packed.shape[1]
    grouped = packed.reshape(copy_count, 1, CAP, feature_width)
    arrived = lax.all_to_all(
        jnp.broadcast_to(grouped, (copy_count, sub_count, CAP, feature_width)).reshape(
            slot_count, CAP, feature_width
        ),
        "slot",
        split_axis=0,
        concat_axis=0,
        tiled=True,
    )
    flat_rows = arrived.reshape(-1, arrived.shape[2])
    hidden = jax.nn.silu(jnp.dot(flat_rows, up_matrix, preferred_element_type=jnp.float32)).astype(
        jnp.bfloat16
    )
    result = jnp.dot(hidden, down_matrix, preferred_element_type=jnp.float32)
    partial_value = result.reshape(slot_count, arrived.shape[1], result.shape[1])
    returned = lax.all_to_all(partial_value, "slot", split_axis=0, concat_axis=0, tiled=True)
    feature_width = returned.shape[2]
    merged = jnp.sum(returned.reshape(copy_count, sub_count, CAP, feature_width), axis=1)
    merged = merged.reshape(copy_count * CAP, feature_width)
    mixed = lax.dot_general(
        scaled,
        merged,
        (((0,), (0,)), ((), ())),
        precision=lax.Precision.HIGHEST,
        preferred_element_type=jnp.float32,
    )
    mixed = lax.psum_scatter(mixed, "tensor", scatter_dimension=1, tiled=True)
    return mixed.astype(jnp.bfloat16)


def solution(mesh):
    body = fused if mesh.shape["slot"] == 2 * E else shards
    return jax.shard_map(
        body,
        mesh=mesh,
        in_specs=(
            P(("groups", "slot"), "tensor"),
            P(("groups", "slot"), None),
            P(("groups", "slot"), None),
            P("slot", None, "tensor"),
            P("slot", "tensor", None),
        ),
        out_specs=P(("groups", "slot"), "tensor"),
        check_vma=False,
    )
```

```python
import functools

import jax
import jax.numpy as jnp
from jax import lax
from jax.experimental import pallas as pl
from jax.experimental.pallas import tpu as pltpu
from jax.sharding import PartitionSpec as P

E = 4
CAP = 24
MOST = 48
WIDTH = 256
UP_SLOTS = 4
UP_TILE = 2048
MESH = pl.DeviceIdType.MESH


def fused_kernel(
    tok_ref, ids_ref, weight_ref, up_hbm, down_hbm, out_ref,
    packed, x_own, x_sib, up_buf, down_buf, acc, hid, part_out, part_own, part_in, summed, returned,
    turned_first, turned_second, gates,
    up_sem, down_sem, go_send, go_recv, fwd_send, fwd_recv, part_send, part_recv, back_send, back_recv,
):
    tok_rows, half = tok_ref.shape
    chunks = half // WIDTH
    rows = E * MOST
    hidden_units = acc.shape[1]
    slot = lax.axis_index("slot")
    core = lax.axis_index("tensor")
    mine = slot // 2
    lane = lax.rem(slot, 2)
    sibling = 1 - core

    def up_copies(c):
        place = lax.rem(c, UP_SLOTS)
        return [
            pltpu.make_async_copy(
                up_hbm.at[0, pl.ds(pl.multiple_of(side * half + c * WIDTH, WIDTH), WIDTH), :],
                up_buf.at[place, i],
                up_sem.at[place, i],
            )
            for i, side in enumerate((core, sibling))
        ]

    def down_copies(c):
        return [
            pltpu.make_async_copy(
                down_hbm.at[0, :, pl.ds(pl.multiple_of(side * half + c * WIDTH, WIDTH), WIDTH)],
                down_buf.at[c, i],
                down_sem.at[c, i],
            )
            for i, side in enumerate((sibling, core))
        ]

    def peer(k):
        return lax.rem(mine + k, E)

    def go_copy(c, k):
        return pltpu.make_async_remote_copy(
            src_ref=packed.at[c, peer(k)],
            dst_ref=x_own.at[c, mine],
            send_sem=go_send.at[c, k - 1],
            recv_sem=go_recv.at[c, k - 1],
            device_id={"slot": peer(k) * 2 + lane},
            device_id_type=MESH,
        )

    def fwd_copy(c):
        return pltpu.make_async_remote_copy(
            src_ref=x_own.at[c],
            dst_ref=x_sib.at[c],
            send_sem=fwd_send.at[c],
            recv_sem=fwd_recv.at[c],
            device_id={"tensor": sibling},
            device_id_type=MESH,
        )

    def part_copy(c):
        return pltpu.make_async_remote_copy(
            src_ref=part_out.at[c],
            dst_ref=part_in.at[c],
            send_sem=part_send.at[c],
            recv_sem=part_recv.at[c],
            device_id={"tensor": sibling},
            device_id_type=MESH,
        )

    def back_copy(c, k):
        return pltpu.make_async_remote_copy(
            src_ref=summed.at[c, peer(k)],
            dst_ref=returned.at[c, mine],
            send_sem=back_send.at[c, k - 1],
            recv_sem=back_recv.at[c, k - 1],
            device_id={"slot": peer(k) * 2 + lane},
            device_id_type=MESH,
        )

    barrier = pltpu.get_barrier_semaphore()
    for k in range(1, E):
        pl.semaphore_signal(barrier, inc=1, device_id={"slot": peer(k) * 2 + lane}, device_id_type=MESH)
    pl.semaphore_signal(barrier, inc=1, device_id={"tensor": sibling}, device_id_type=MESH)

    for c in range(UP_SLOTS):
        for copy in up_copies(c):
            copy.start()

    first, second = ids_ref[0:1, :], ids_ref[1:2, :]
    experts = lax.broadcasted_iota(jnp.int32, (2 * E, tok_rows), 0)
    is_first = jnp.where(experts == first, 1.0, 0.0)
    is_second = jnp.where(experts == second, 1.0, 0.0)
    before = jnp.where(
        lax.broadcasted_iota(jnp.int32, (tok_rows, tok_rows), 0)
        < lax.broadcasted_iota(jnp.int32, (tok_rows, tok_rows), 1),
        1.0,
        0.0,
    ).astype(jnp.bfloat16)
    rank = jnp.dot((is_first + is_second).astype(jnp.bfloat16), before, preferred_element_type=jnp.float32)
    place = rank + (experts * MOST).astype(jnp.float32)
    places = lax.broadcasted_iota(jnp.int32, (rows, tok_rows), 0).astype(jnp.float32)
    one_first = jnp.where(places == jnp.sum(is_first * place, axis=0, keepdims=True), 1.0, 0.0)
    one_second = jnp.where(places == jnp.sum(is_second * place, axis=0, keepdims=True), 1.0, 0.0)
    chosen = (one_first + one_second).astype(jnp.bfloat16)

    for c in range(chunks):
        piece = jnp.dot(
            chosen, tok_ref[:, c * WIDTH : (c + 1) * WIDTH], preferred_element_type=jnp.float32
        ).astype(jnp.bfloat16)
        packed[c] = piece.reshape(E, MOST, WIDTH)
        if c == 0:
            pl.semaphore_wait(barrier, E)
        for k in range(1, E):
            go_copy(c, k).start()
    for c in range(chunks):
        x_own[c, mine] = packed[c, mine]

    turned_first[...] = one_first.T.astype(jnp.bfloat16)
    turned_second[...] = one_second.T.astype(jnp.bfloat16)
    gates[0] = jnp.broadcast_to(weight_ref[0:1, :], (128, tok_rows)).T
    gates[1] = jnp.broadcast_to(weight_ref[1:2, :], (128, tok_rows)).T

    def arrive(c):
        for k in range(1, E):
            go_copy(c, k).wait_recv()
        fwd_copy(c).start()

    def up_step(c, own, other):
        if own:
            up_copies(c)[0].wait()
            left = x_own[c].reshape(rows, WIDTH)
            spot = lax.rem(c, UP_SLOTS)
        if other:
            fwd_copy(c - 1).wait_recv()
            up_copies(c - 1)[1].wait()
            right = x_sib[c - 1].reshape(rows, WIDTH)
            last = lax.rem(c - 1, UP_SLOTS)

        @pl.loop(0, hidden_units // UP_TILE)
        def _(n):
            at = pl.ds(pl.multiple_of(n * UP_TILE, UP_TILE), UP_TILE)
            value = None
            if own:
                value = jnp.dot(left, up_buf[spot, 0, :, at], preferred_element_type=jnp.float32)
            if other:
                more = jnp.dot(right, up_buf[last, 1, :, at], preferred_element_type=jnp.float32)
                value = more if value is None else value + more
                value += acc[:, at]
            if own:
                acc[:, at] = value
            else:
                hid[:, at] = (value / (1.0 + jnp.exp(-value))).astype(jnp.bfloat16)

        if own:
            for copy in down_copies(c):
                copy.start()

    arrive(0)
    up_step(0, True, False)
    up_copies(UP_SLOTS)[0].start()

    @pl.loop(1, chunks)
    def _(c):
        arrive(c)
        up_step(c, True, True)

        @pl.when(c + UP_SLOTS < chunks)
        def _():
            up_copies(c + UP_SLOTS)[0].start()

        @pl.when(c - 1 + UP_SLOTS < chunks)
        def _():
            up_copies(c - 1 + UP_SLOTS)[1].start()

    up_step(chunks, False, True)

    def finish(c):
        part_copy(c).wait_recv()
        total = (part_own[c] + part_in[c]).astype(jnp.bfloat16)
        summed[c] = total.reshape(E, MOST, WIDTH)
        for k in range(1, E):
            back_copy(c, k).start()
        returned[c, mine] = summed[c, mine]

    @pl.loop(0, chunks)
    def _(c):
        for copy in down_copies(c):
            copy.wait()
        part_out[c] = jnp.dot(hid[...], down_buf[c, 0], preferred_element_type=jnp.float32)
        part_copy(c).start()

        @pl.when(c > 0)
        def _():
            finish(c - 1)

        part_own[c] = jnp.dot(hid[...], down_buf[c, 1], preferred_element_type=jnp.float32)

    finish(chunks - 1)

    for c in range(chunks):
        for k in range(1, E):
            back_copy(c, k).wait_recv()
        block = returned[c].reshape(rows, WIDTH)
        value = gates[0, :, 0:1] * jnp.dot(turned_first[...], block, preferred_element_type=jnp.float32)
        value += gates[1, :, 0:1] * jnp.dot(turned_second[...], block, preferred_element_type=jnp.float32)
        out_ref[:, c * WIDTH : (c + 1) * WIDTH] = value.astype(jnp.bfloat16)

    for c in range(chunks):
        fwd_copy(c).wait_send()
        part_copy(c).wait_send()
        for k in range(1, E):
            go_copy(c, k).wait_send()
            back_copy(c, k).wait_send()


def fused(tokens, expert_ids, route_weights, up_weight, down_weight):
    tok_rows, half = tokens.shape
    hidden_units = up_weight.shape[2]
    chunks = half // WIDTH
    rows = E * MOST
    vmem = pl.BlockSpec(memory_space=pltpu.VMEM)
    hbm = pl.BlockSpec(memory_space=pl.ANY)
    sems = lambda *shape: pltpu.SemaphoreType.DMA(shape)
    blocks = pltpu.VMEM((chunks, E, MOST, WIDTH), jnp.bfloat16)
    wide = pltpu.VMEM((chunks, rows, WIDTH), jnp.float32)
    return pl.pallas_call(
        fused_kernel,
        out_shape=jax.ShapeDtypeStruct((tok_rows, half), jnp.bfloat16),
        in_specs=[vmem, vmem, vmem, hbm, hbm],
        out_specs=vmem,
        scratch_shapes=[
            blocks,
            blocks,
            blocks,
            pltpu.VMEM((UP_SLOTS, 2, WIDTH, hidden_units), jnp.bfloat16),
            pltpu.VMEM((chunks, 2, hidden_units, WIDTH), jnp.bfloat16),
            pltpu.VMEM((rows, hidden_units), jnp.float32),
            pltpu.VMEM((rows, hidden_units), jnp.bfloat16),
            wide,
            wide,
            wide,
            blocks,
            blocks,
            pltpu.VMEM((tok_rows, rows), jnp.bfloat16),
            pltpu.VMEM((tok_rows, rows), jnp.bfloat16),
            pltpu.VMEM((2, tok_rows, 128), jnp.float32),
            sems(UP_SLOTS, 2),
            sems(chunks, 2),
            sems(chunks, E - 1),
            sems(chunks, E - 1),
            sems(chunks),
            sems(chunks),
            sems(chunks),
            sems(chunks),
            sems(chunks, E - 1),
            sems(chunks, E - 1),
        ],
        compiler_params=pltpu.CompilerParams(
            collective_id=0, has_side_effects=True, vmem_limit_bytes=60 * 1024 * 1024
        ),
        cost_estimate=pl.CostEstimate(
            flops=8 * rows * half * hidden_units,
            bytes_accessed=8 * half * hidden_units,
            transcendentals=rows * hidden_units,
        ),
    )(tokens, expert_ids.T, route_weights.T, up_weight, down_weight)


def shards(tokens, expert_ids, route_weights, up_weight, down_weight):
    slot_count = lax.axis_size("slot")
    tok_rows = tokens.shape[0]
    copy_count = 2 * E
    sub_count = slot_count // copy_count
    up_matrix = up_weight[0]
    down_matrix = down_weight[0]
    flat_ids = expert_ids.reshape(-1)
    one_hot = (flat_ids[:, None] == jnp.arange(E, dtype=jnp.int32)[None, :]).astype(jnp.int32)
    route_rank = jnp.sum(one_hot * (jnp.cumsum(one_hot, axis=0) - 1), axis=1)
    overflow = (route_rank >= CAP).astype(jnp.int32)
    target = ((2 * flat_ids + overflow) * CAP + route_rank - overflow * CAP).reshape(
        tok_rows, expert_ids.shape[1]
    )
    positions = jnp.arange(copy_count * CAP, dtype=jnp.int32)
    matches = target[None, :, :] == positions[:, None, None]
    chosen = jnp.sum(matches.astype(jnp.float32), axis=2).astype(jnp.bfloat16)
    scaled = jnp.sum(
        jnp.where(matches, route_weights[None, :, :], jnp.zeros_like(route_weights)[None, :, :]),
        axis=2,
    )
    gathered = lax.all_gather(tokens, "tensor", axis=1, tiled=True)
    packed = jnp.dot(chosen, gathered, preferred_element_type=jnp.float32).astype(jnp.bfloat16)
    feature_width = packed.shape[1]
    grouped = packed.reshape(copy_count, 1, CAP, feature_width)
    arrived = lax.all_to_all(
        jnp.broadcast_to(grouped, (copy_count, sub_count, CAP, feature_width)).reshape(
            slot_count, CAP, feature_width
        ),
        "slot",
        split_axis=0,
        concat_axis=0,
        tiled=True,
    )
    flat_rows = arrived.reshape(-1, arrived.shape[2])
    hidden = jax.nn.silu(jnp.dot(flat_rows, up_matrix, preferred_element_type=jnp.float32)).astype(
        jnp.bfloat16
    )
    result = jnp.dot(hidden, down_matrix, preferred_element_type=jnp.float32)
    partial_value = result.reshape(slot_count, arrived.shape[1], result.shape[1])
    returned = lax.all_to_all(partial_value, "slot", split_axis=0, concat_axis=0, tiled=True)
    feature_width = returned.shape[2]
    merged = jnp.sum(returned.reshape(copy_count, sub_count, CAP, feature_width), axis=1)
    merged = merged.reshape(copy_count * CAP, feature_width)
    mixed = lax.dot_general(
        scaled,
        merged,
        (((0,), (0,)), ((), ())),
        precision=lax.Precision.HIGHEST,
        preferred_element_type=jnp.float32,
    )
    mixed = lax.psum_scatter(mixed, "tensor", scatter_dimension=1, tiled=True)
    return mixed.astype(jnp.bfloat16)


def solution(mesh):
    body = fused if mesh.shape["slot"] == 2 * E else shards
    return jax.shard_map(
        body,
        mesh=mesh,
        in_specs=(
            P(("groups", "slot"), "tensor"),
            P(("groups", "slot"), None),
            P(("groups", "slot"), None),
            P("slot", None, "tensor"),
            P("slot", "tensor", None),
        ),
        out_specs=P(("groups", "slot"), "tensor"),
        check_vma=False,
    )
```

```python
import functools

import jax
import jax.numpy as jnp
from jax import lax
from jax.experimental import pallas as pl
from jax.experimental.pallas import tpu as pltpu
from jax.sharding import PartitionSpec as P

E = 4
CAP = 24
MOST = 48
WIDTH = 256
UP_SLOTS = 4
UP_TILE = 4096
MESH = pl.DeviceIdType.MESH


def fused_kernel(
    tok_ref, ids_ref, weight_ref, up_hbm, down_hbm, out_ref,
    packed, x_own, x_sib, up_buf, down_buf, acc, hid, part_out, part_own, part_in, summed, returned,
    turned_first, turned_second, gates,
    up_sem, down_sem, go_send, go_recv, fwd_send, fwd_recv, part_send, part_recv, back_send, back_recv,
):
    tok_rows, half = tok_ref.shape
    chunks = half // WIDTH
    rows = E * MOST
    hidden_units = acc.shape[1]
    slot = lax.axis_index("slot")
    core = lax.axis_index("tensor")
    mine = slot // 2
    lane = lax.rem(slot, 2)
    sibling = 1 - core

    def up_copies(c):
        place = lax.rem(c, UP_SLOTS)
        return [
            pltpu.make_async_copy(
                up_hbm.at[0, pl.ds(pl.multiple_of(side * half + c * WIDTH, WIDTH), WIDTH), :],
                up_buf.at[place, i],
                up_sem.at[place, i],
            )
            for i, side in enumerate((core, sibling))
        ]

    def down_copies(c):
        return [
            pltpu.make_async_copy(
                down_hbm.at[0, :, pl.ds(pl.multiple_of(side * half + c * WIDTH, WIDTH), WIDTH)],
                down_buf.at[c, i],
                down_sem.at[c, i],
            )
            for i, side in enumerate((sibling, core))
        ]

    def peer(k):
        return lax.rem(mine + k, E)

    def go_copy(c, k):
        return pltpu.make_async_remote_copy(
            src_ref=packed.at[c, peer(k)],
            dst_ref=x_own.at[c, mine],
            send_sem=go_send.at[c, k - 1],
            recv_sem=go_recv.at[c, k - 1],
            device_id={"slot": peer(k) * 2 + lane},
            device_id_type=MESH,
        )

    def fwd_copy(c):
        return pltpu.make_async_remote_copy(
            src_ref=x_own.at[c],
            dst_ref=x_sib.at[c],
            send_sem=fwd_send.at[c],
            recv_sem=fwd_recv.at[c],
            device_id={"tensor": sibling},
            device_id_type=MESH,
        )

    def part_copy(c):
        return pltpu.make_async_remote_copy(
            src_ref=part_out.at[c],
            dst_ref=part_in.at[c],
            send_sem=part_send.at[c],
            recv_sem=part_recv.at[c],
            device_id={"tensor": sibling},
            device_id_type=MESH,
        )

    def back_copy(c, k):
        return pltpu.make_async_remote_copy(
            src_ref=summed.at[c, peer(k)],
            dst_ref=returned.at[c, mine],
            send_sem=back_send.at[c, k - 1],
            recv_sem=back_recv.at[c, k - 1],
            device_id={"slot": peer(k) * 2 + lane},
            device_id_type=MESH,
        )

    barrier = pltpu.get_barrier_semaphore()
    for k in range(1, E):
        pl.semaphore_signal(barrier, inc=1, device_id={"slot": peer(k) * 2 + lane}, device_id_type=MESH)
    pl.semaphore_signal(barrier, inc=1, device_id={"tensor": sibling}, device_id_type=MESH)

    for c in range(UP_SLOTS):
        for copy in up_copies(c):
            copy.start()

    first, second = ids_ref[0:1, :], ids_ref[1:2, :]
    experts = lax.broadcasted_iota(jnp.int32, (2 * E, tok_rows), 0)
    is_first = jnp.where(experts == first, 1.0, 0.0)
    is_second = jnp.where(experts == second, 1.0, 0.0)
    before = jnp.where(
        lax.broadcasted_iota(jnp.int32, (tok_rows, tok_rows), 0)
        < lax.broadcasted_iota(jnp.int32, (tok_rows, tok_rows), 1),
        1.0,
        0.0,
    ).astype(jnp.bfloat16)
    rank = jnp.dot((is_first + is_second).astype(jnp.bfloat16), before, preferred_element_type=jnp.float32)
    place = rank + (experts * MOST).astype(jnp.float32)
    places = lax.broadcasted_iota(jnp.int32, (rows, tok_rows), 0).astype(jnp.float32)
    one_first = jnp.where(places == jnp.sum(is_first * place, axis=0, keepdims=True), 1.0, 0.0)
    one_second = jnp.where(places == jnp.sum(is_second * place, axis=0, keepdims=True), 1.0, 0.0)
    chosen = (one_first + one_second).astype(jnp.bfloat16)

    for c in range(chunks):
        piece = jnp.dot(
            chosen, tok_ref[:, c * WIDTH : (c + 1) * WIDTH], preferred_element_type=jnp.float32
        ).astype(jnp.bfloat16)
        packed[c] = piece.reshape(E, MOST, WIDTH)
        if c == 0:
            pl.semaphore_wait(barrier, E)
        for k in range(1, E):
            go_copy(c, k).start()
    for c in range(chunks):
        x_own[c, mine] = packed[c, mine]

    turned_first[...] = one_first.T.astype(jnp.bfloat16)
    turned_second[...] = one_second.T.astype(jnp.bfloat16)
    gates[0] = jnp.broadcast_to(weight_ref[0:1, :], (128, tok_rows)).T
    gates[1] = jnp.broadcast_to(weight_ref[1:2, :], (128, tok_rows)).T

    def arrive(c):
        for k in range(1, E):
            go_copy(c, k).wait_recv()
        fwd_copy(c).start()

    def up_step(c, own, other):
        if own:
            up_copies(c)[0].wait()
            left = x_own[c].reshape(rows, WIDTH)
            spot = lax.rem(c, UP_SLOTS)
        if other:
            fwd_copy(c - 1).wait_recv()
            up_copies(c - 1)[1].wait()
            right = x_sib[c - 1].reshape(rows, WIDTH)
            last = lax.rem(c - 1, UP_SLOTS)

        @pl.loop(0, hidden_units // UP_TILE)
        def _(n):
            at = pl.ds(pl.multiple_of(n * UP_TILE, UP_TILE), UP_TILE)
            value = None
            if own:
                value = jnp.dot(left, up_buf[spot, 0, :, at], preferred_element_type=jnp.float32)
            if other:
                more = jnp.dot(right, up_buf[last, 1, :, at], preferred_element_type=jnp.float32)
                value = more if value is None else value + more
                value += acc[:, at]
            if own:
                acc[:, at] = value
            else:
                hid[:, at] = (value / (1.0 + jnp.exp(-value))).astype(jnp.bfloat16)

        if own:
            for copy in down_copies(c):
                copy.start()

    arrive(0)
    up_step(0, True, False)
    up_copies(UP_SLOTS)[0].start()

    @pl.loop(1, chunks)
    def _(c):
        arrive(c)
        up_step(c, True, True)

        @pl.when(c + UP_SLOTS < chunks)
        def _():
            up_copies(c + UP_SLOTS)[0].start()

        @pl.when(c - 1 + UP_SLOTS < chunks)
        def _():
            up_copies(c - 1 + UP_SLOTS)[1].start()

    up_step(chunks, False, True)

    def finish(c):
        part_copy(c).wait_recv()
        total = (part_own[c] + part_in[c]).astype(jnp.bfloat16)
        summed[c] = total.reshape(E, MOST, WIDTH)
        for k in range(1, E):
            back_copy(c, k).start()
        returned[c, mine] = summed[c, mine]

    @pl.loop(0, chunks)
    def _(c):
        for copy in down_copies(c):
            copy.wait()
        part_out[c] = jnp.dot(hid[...], down_buf[c, 0], preferred_element_type=jnp.float32)
        part_copy(c).start()

        @pl.when(c > 0)
        def _():
            finish(c - 1)

        part_own[c] = jnp.dot(hid[...], down_buf[c, 1], preferred_element_type=jnp.float32)

    finish(chunks - 1)

    for c in range(chunks):
        for k in range(1, E):
            back_copy(c, k).wait_recv()
        block = returned[c].reshape(rows, WIDTH)
        value = gates[0, :, 0:1] * jnp.dot(turned_first[...], block, preferred_element_type=jnp.float32)
        value += gates[1, :, 0:1] * jnp.dot(turned_second[...], block, preferred_element_type=jnp.float32)
        out_ref[:, c * WIDTH : (c + 1) * WIDTH] = value.astype(jnp.bfloat16)

    for c in range(chunks):
        fwd_copy(c).wait_send()
        part_copy(c).wait_send()
        for k in range(1, E):
            go_copy(c, k).wait_send()
            back_copy(c, k).wait_send()


def fused(tokens, expert_ids, route_weights, up_weight, down_weight):
    tok_rows, half = tokens.shape
    hidden_units = up_weight.shape[2]
    chunks = half // WIDTH
    rows = E * MOST
    vmem = pl.BlockSpec(memory_space=pltpu.VMEM)
    hbm = pl.BlockSpec(memory_space=pl.ANY)
    sems = lambda *shape: pltpu.SemaphoreType.DMA(shape)
    blocks = pltpu.VMEM((chunks, E, MOST, WIDTH), jnp.bfloat16)
    wide = pltpu.VMEM((chunks, rows, WIDTH), jnp.float32)
    return pl.pallas_call(
        fused_kernel,
        out_shape=jax.ShapeDtypeStruct((tok_rows, half), jnp.bfloat16),
        in_specs=[vmem, vmem, vmem, hbm, hbm],
        out_specs=vmem,
        scratch_shapes=[
            blocks,
            blocks,
            blocks,
            pltpu.VMEM((UP_SLOTS, 2, WIDTH, hidden_units), jnp.bfloat16),
            pltpu.VMEM((chunks, 2, hidden_units, WIDTH), jnp.bfloat16),
            pltpu.VMEM((rows, hidden_units), jnp.float32),
            pltpu.VMEM((rows, hidden_units), jnp.bfloat16),
            wide,
            wide,
            wide,
            blocks,
            blocks,
            pltpu.VMEM((tok_rows, rows), jnp.bfloat16),
            pltpu.VMEM((tok_rows, rows), jnp.bfloat16),
            pltpu.VMEM((2, tok_rows, 128), jnp.float32),
            sems(UP_SLOTS, 2),
            sems(chunks, 2),
            sems(chunks, E - 1),
            sems(chunks, E - 1),
            sems(chunks),
            sems(chunks),
            sems(chunks),
            sems(chunks),
            sems(chunks, E - 1),
            sems(chunks, E - 1),
        ],
        compiler_params=pltpu.CompilerParams(
            collective_id=0, has_side_effects=True, vmem_limit_bytes=60 * 1024 * 1024
        ),
        cost_estimate=pl.CostEstimate(
            flops=8 * rows * half * hidden_units,
            bytes_accessed=8 * half * hidden_units,
            transcendentals=rows * hidden_units,
        ),
    )(tokens, expert_ids.T, route_weights.T, up_weight, down_weight)


def shards(tokens, expert_ids, route_weights, up_weight, down_weight):
    slot_count = lax.axis_size("slot")
    tok_rows = tokens.shape[0]
    copy_count = 2 * E
    sub_count = slot_count // copy_count
    up_matrix = up_weight[0]
    down_matrix = down_weight[0]
    flat_ids = expert_ids.reshape(-1)
    one_hot = (flat_ids[:, None] == jnp.arange(E, dtype=jnp.int32)[None, :]).astype(jnp.int32)
    route_rank = jnp.sum(one_hot * (jnp.cumsum(one_hot, axis=0) - 1), axis=1)
    overflow = (route_rank >= CAP).astype(jnp.int32)
    target = ((2 * flat_ids + overflow) * CAP + route_rank - overflow * CAP).reshape(
        tok_rows, expert_ids.shape[1]
    )
    positions = jnp.arange(copy_count * CAP, dtype=jnp.int32)
    matches = target[None, :, :] == positions[:, None, None]
    chosen = jnp.sum(matches.astype(jnp.float32), axis=2).astype(jnp.bfloat16)
    scaled = jnp.sum(
        jnp.where(matches, route_weights[None, :, :], jnp.zeros_like(route_weights)[None, :, :]),
        axis=2,
    )
    gathered = lax.all_gather(tokens, "tensor", axis=1, tiled=True)
    packed = jnp.dot(chosen, gathered, preferred_element_type=jnp.float32).astype(jnp.bfloat16)
    feature_width = packed.shape[1]
    grouped = packed.reshape(copy_count, 1, CAP, feature_width)
    arrived = lax.all_to_all(
        jnp.broadcast_to(grouped, (copy_count, sub_count, CAP, feature_width)).reshape(
            slot_count, CAP, feature_width
        ),
        "slot",
        split_axis=0,
        concat_axis=0,
        tiled=True,
    )
    flat_rows = arrived.reshape(-1, arrived.shape[2])
    hidden = jax.nn.silu(jnp.dot(flat_rows, up_matrix, preferred_element_type=jnp.float32)).astype(
        jnp.bfloat16
    )
    result = jnp.dot(hidden, down_matrix, preferred_element_type=jnp.float32)
    partial_value = result.reshape(slot_count, arrived.shape[1], result.shape[1])
    returned = lax.all_to_all(partial_value, "slot", split_axis=0, concat_axis=0, tiled=True)
    feature_width = returned.shape[2]
    merged = jnp.sum(returned.reshape(copy_count, sub_count, CAP, feature_width), axis=1)
    merged = merged.reshape(copy_count * CAP, feature_width)
    mixed = lax.dot_general(
        scaled,
        merged,
        (((0,), (0,)), ((), ())),
        precision=lax.Precision.HIGHEST,
        preferred_element_type=jnp.float32,
    )
    mixed = lax.psum_scatter(mixed, "tensor", scatter_dimension=1, tiled=True)
    return mixed.astype(jnp.bfloat16)


def solution(mesh):
    body = fused if mesh.shape["slot"] == 2 * E else shards
    return jax.shard_map(
        body,
        mesh=mesh,
        in_specs=(
            P(("groups", "slot"), "tensor"),
            P(("groups", "slot"), None),
            P(("groups", "slot"), None),
            P("slot", None, "tensor"),
            P("slot", "tensor", None),
        ),
        out_specs=P(("groups", "slot"), "tensor"),
        check_vma=False,
    )
```
